512 devices in a mesh: dp: 16 (over z_lo, core), tensor: 32 (over x, y, z_hi).
Axes of the slice: x: 4, y: 4, z: 16 (z_hi: 2, z_lo: 8; z = z_hi * 8 + z_lo), core: 2. Of those that a mesh axis runs over, the one named last changes fastest.
Arguments:
- acts: bfloat16 [2, 16384, 28672], P(None, 'dp', 'tensor'), may hold values from -6 to 6
- grads: bfloat16 [2, 16384, 8192], P(None, 'dp', 'tensor'), may hold values from -6 to 6
- proj_in: bfloat16 [2, 28672, 64], P(None, 'tensor'), may hold values from -0.03125 to 0.03125
- proj_out: bfloat16 [2, 8192, 64], P(None, 'tensor'), may hold values from -0.0625 to 0.0625
- queries: bfloat16 [1024, 8192], P('dp', 'tensor'), may hold values from -0.0078125 to 0.0078125
- lengths: int32 [64], P('dp'), may hold values from 32 to 256, as said below
- loss_mask: int32 [64, 256], P('dp'), may hold values 0 or 1
Outputs:
- scores: float32 [64, 1024], P('dp', 'tensor')
The draws below stay inside these ranges and needn't reach their ends.
Inputs may be any that keep to these rules, and one draw needn't show every extreme that they name: `lengths`: each length lies between 32 and 256, and at least one sequence has all 256 slots live.
All inputs are finite; a program needn't handle non-finite values. No bound on the sum of `loss_mask` on one device may be relied on, other than what follows from the above.
Results may differ from the reference program's by a relative error of at most 0.0029.
Values may be sent and summed in bfloat16 or wider, within the bound.
A program may use at most 64 MiB of HBM per device.

```python
import jax
import jax.numpy as jnp
from jax import lax

D = 8192
FF = 28672
R = 64
LAYERS = 2
LEN = 256
SEQS = 64
TOKENS = 16384
QUERIES = 1024


def draw_lengths(key, part):
    key = jax.random.fold_in(key, 11)
    first, second = jax.random.split(key)
    values = jax.random.randint(first, (SEQS,), LEN // 8, LEN + 1, dtype=jnp.int32)
    chosen = jax.random.randint(second, (), 0, SEQS, dtype=jnp.int32)
    return jnp.where(jnp.arange(SEQS, dtype=jnp.int32) == chosen, LEN, values).astype(jnp.int32)


def with_ends(drawn, rng, smallest, largest):
    longest = drawn.shape.index(max(drawn.shape))
    spots = []
    for shift in (0, 1):
        where = [jax.random.randint(jax.random.fold_in(rng, axis), (), 0, length) for axis, length in enumerate(drawn.shape)]
        where[longest] = (where[longest] + shift) % drawn.shape[longest]
        spots.append(tuple(where))
    return drawn.at[spots[0]].set(smallest).at[spots[1]].set(largest)


def with_spikes(entries, key, source, target, blocks, factor):
    def block_of(dim):
        return (jnp.arange(entries.shape[dim]) // (entries.shape[dim] // blocks)).reshape((-1,) + (1,) * (entries.ndim - 1 - dim))

    first = jax.random.permutation(key, blocks)[block_of(target)]
    far = (block_of(target) + blocks // 2) % blocks
    return jnp.where((block_of(source) == first) | (block_of(source) == far), factor * entries, entries)


def levels(stream_key, shape, cuts, smallest, high):
    def one(dim, parts):
        heights = jax.random.uniform(jax.random.fold_in(jax.random.fold_in(stream_key, 6), dim), (parts,), jnp.float32, smallest / len(cuts), high / len(cuts))
        return jnp.repeat(jnp.exp(heights), shape[dim] // parts).reshape((-1,) + (1,) * (len(shape) - dim - 1))

    gain = one(*cuts[0])
    for cut in cuts[1:]:
        gain = gain * one(*cut)
    return gain


def gaussian(stream_key, extent, scale, bound, cuts=(), kind=jnp.bfloat16):
    drawn = scale * jax.random.normal(stream_key, extent, jnp.float32)
    if cuts:
        drawn = drawn * levels(stream_key, extent, cuts, -0.22, 0.18)
    return jnp.clip(drawn, -bound, bound).astype(kind)


def bell_draw_with(own_key, extent, spread, most, cuts, heavy, kind=jnp.bfloat16):
    values = spread * jax.random.normal(own_key, extent, jnp.float32)
    if cuts:
        values = values * levels(own_key, extent, cuts, -0.22, 0.18)
    return jnp.clip(with_spikes(values, jax.random.fold_in(own_key, 3), *heavy), -most, most).astype(kind)


def setup_inputs(seed: int = 0) -> dict:
    arg_keys = jax.random.split(jax.random.key(seed), 8)
    return {
        "acts": gaussian(arg_keys[0], (LAYERS, TOKENS, FF), 1.0, 6.0, ((1, 16), (2, 32))),
        "grads": gaussian(arg_keys[1], (LAYERS, TOKENS, D), 1.0, 6.0, ((1, 16), (2, 32))),
        "proj_in": gaussian(arg_keys[2], (LAYERS, FF, R), FF ** -0.5, 0.03125, ((1, 32),)),
        "proj_out": gaussian(arg_keys[3], (LAYERS, D, R), D ** -0.5, 0.0625, ((1, 32),)),
        "queries": bell_draw_with(arg_keys[4], (QUERIES, LAYERS * R * R), (LAYERS * R * R * LEN) ** -0.5, 0.0078125, ((0, 16), (1, 32)), (1, 0, 32, 2.75)),
        "lengths": draw_lengths(jax.random.fold_in(arg_keys[7], 71), 0),
        "loss_mask": with_ends((jax.random.randint(arg_keys[6], (SEQS, LEN), 0, 4) < 3).astype(jnp.int32), jax.random.fold_in(arg_keys[6], 1), 0, 1),
    }


def reference(acts, grads, proj_in, proj_out, queries, lengths, loss_mask):
    slots = jnp.arange(LEN, dtype=jnp.int32)
    live = jnp.where(slots[None, :] < lengths[:, None], loss_mask, 0).astype(jnp.float32)
    live = live.reshape(SEQS * LEN, 1)
    pieces = []
    for layer in range(LAYERS):
        inner = jnp.dot(acts[layer], proj_in[layer], preferred_element_type=jnp.float32)
        outer = jnp.dot(grads[layer], proj_out[layer], preferred_element_type=jnp.float32) * live
        kron = jnp.einsum("sta,stb->sab", outer.reshape(SEQS, LEN, R), inner.reshape(SEQS, LEN, R),
                          precision=lax.Precision.HIGHEST)
        pieces.append(kron.reshape(SEQS, R * R))
    flat = jnp.concatenate(pieces, axis=1).astype(jnp.bfloat16)
    return jnp.dot(flat, queries.T, preferred_element_type=jnp.float32)
```

```python
import jax
import jax.numpy as jnp
from jax import lax
from jax.experimental import pallas as pl
from jax.experimental.pallas import tpu as pltpu
from jax.sharding import PartitionSpec as P

MESH = pl.DeviceIdType.MESH
F32 = jnp.float32
BF16 = jnp.bfloat16


def kernel(acts, grads, pin, pout, qry, lens, mask, out,
           av, gv, piv, pov, part, got, zsum, zgot, ksend, kgot, qall, ssend, sgot,
           load_sem, w_sem, own_sem, rs_send, rs_recv, q_send, q_recv, c_send, c_recv,
           z_send, z_recv, k_send, k_recv, s_send, s_recv):
    d = lax.axis_index("dp")
    t = lax.axis_index("tensor")
    zl, c = d // 2, d % 2
    u, zh = t // 2, t % 2
    x, y = u // 4, u % 4
    z = zh * 8 + zl

    def plane(index):
        return {"dp": d, "tensor": 2 * index + zh}

    def around(k):
        return ((x + k // 4) % 4) * 4 + (y + k % 4) % 4

    def column(k):
        zz = (z + k) % 16
        return {"dp": 2 * (zz % 8) + c, "tensor": 2 * u + zz // 8}

    sibling = {"dp": 2 * zl + 1 - c, "tensor": t}
    across = {"dp": d, "tensor": 2 * u + 1 - zh}

    def remote(src, dst, send, recv, where):
        pltpu.make_async_remote_copy(
            src_ref=src, dst_ref=dst, send_sem=send, recv_sem=recv, device_id=where, device_id_type=MESH
        ).start()

    def wait(ref, sem):
        pltpu.make_async_copy(ref, ref, sem).wait()

    def loads(i):
        layer, seq = i // 4, i % 4
        rows = pl.ds(pl.multiple_of(seq * 256, 256), 256)
        return (
            pltpu.make_async_copy(acts.at[layer, rows], av.at[i], load_sem.at[0, i]),
            pltpu.make_async_copy(grads.at[layer, rows], gv.at[i], load_sem.at[1, i]),
        )

    load_pin = pltpu.make_async_copy(pin, piv, w_sem.at[0])
    load_pout = pltpu.make_async_copy(pout, pov, w_sem.at[1])
    load_pin.start()
    load_pout.start()

    def start_load(i, carry):
        for copy in loads(i):
            copy.start()
        return carry

    lax.fori_loop(0, 8, start_load, 0)
    own_q = pltpu.make_async_copy(
        qry.at[pl.ds(pl.multiple_of(32 * zh, 32), 32)], qall.at[(2 * c + zh) * 8 + zl], own_sem
    )
    own_q.start()

    barrier = pltpu.get_barrier_semaphore()

    def greet(k, carry):
        pl.semaphore_signal(barrier, inc=1, device_id=column(k), device_id_type=MESH)
        pl.semaphore_signal(barrier, inc=1, device_id=plane(around(k)), device_id_type=MESH)
        return carry

    lax.fori_loop(1, 16, greet, 0)
    pl.semaphore_signal(barrier, inc=1, device_id=sibling, device_id_type=MESH)

    load_pin.wait()
    load_pout.wait()

    def project(i, carry):
        for copy in loads(i):
            copy.wait()
        layer = i // 4
        inner = jnp.dot(av[i], piv[layer], preferred_element_type=F32)
        outer = jnp.dot(gv[i], pov[layer], preferred_element_type=F32)
        part[2 * i, :, 0:64] = inner[:128]
        part[2 * i + 1, :, 0:64] = inner[128:]
        part[2 * i, :, 64:128] = outer[:128]
        part[2 * i + 1, :, 64:128] = outer[128:]
        return carry

    lax.fori_loop(0, 8, project, 0)
    pl.semaphore_wait(barrier, 31)

    for h in range(2):
        rows = pl.ds(64 * h, 64)

        def scatter(k, carry):
            to = around(k)
            remote(part.at[to, rows], got.at[h, k - 1], rs_send.at[h], rs_recv.at[h], plane(to))
            return carry

        lax.fori_loop(1, 16, scatter, 0)
        if h == 0:

            def spread(k, carry):
                far = (z + k) % 16 // 8
                remote(qry.at[pl.ds(pl.multiple_of(32 * far, 32), 32)], qall.at[(2 * c + zh) * 8 + zl], q_send, q_recv, column(k))
                return carry

            lax.fori_loop(1, 16, spread, 0)

    for h in range(2):
        wait(got.at[h], rs_recv.at[h])
        total = part[u, 64 * h : 64 * h + 64]
        for k in range(15):
            total = total + got[h, k]
        zsum[h] = total
        remote(zsum.at[h], zgot.at[h], z_send.at[h], z_recv.at[h], across)

    own_q.wait()
    wait(qall.at[0:15], q_recv)
    core_half = qall.at[pl.ds(16 * c, 16)]
    remote(core_half, core_half, c_send, c_recv, sibling)

    seq, half = (u // 2) % 4, u % 2
    slots = lax.broadcasted_iota(jnp.int32, (1, 128), 1) + half * 128
    pair = jnp.where(half == 0, mask[:, :128], mask[:, 128:])
    row = lax.broadcasted_iota(jnp.int32, (4, 128), 0)
    counted = jnp.sum(jnp.where(row == seq, pair, 0), axis=0, keepdims=True)
    live = jnp.where(slots < lens[seq], counted, 0).astype(F32)
    lane = lax.broadcasted_iota(jnp.int32, (128, 128), 1)

    for h in range(2):
        wait(zgot.at[h], z_recv.at[h])
    unit = jnp.concatenate([zsum[0] + zgot[0], zsum[1] + zgot[1]], axis=0)
    weighted = unit.T[64:128] * live
    twice = jnp.where(lane < 64, unit, pltpu.roll(unit, 64, 1))
    kron = jnp.dot(weighted, twice, precision=lax.Precision.HIGHEST, preferred_element_type=F32)
    ksend[...] = kron.reshape(8, 8, 128)
    mine = u % 8

    def hand(k, carry):
        to = (mine + k) % 8
        remote(ksend.at[to], kgot.at[mine], k_send, k_recv, plane((u // 8) * 8 + to))
        return carry

    lax.fori_loop(1, 8, hand, 0)
    kgot[mine] = ksend[mine]
    wait(qall.at[0:16], c_recv)
    wait(kgot.at[0:7], k_recv)
    rows8 = []
    for s in range(4):
        rows8.append(kgot[2 * s] + kgot[2 * s + 1])
    stacked = jnp.stack(rows8, axis=0)
    low = lax.broadcasted_iota(jnp.int32, (4, 128), 1) < 64
    flat = jnp.concatenate(
        [jnp.where(low, stacked[:, 2 * r, :], stacked[:, 2 * r + 1, :]) for r in range(4)], axis=1
    )
    flat = jnp.concatenate([flat, jnp.zeros_like(flat)], axis=0).astype(BF16)
    nt = (((1,), (1,)), ((), ()))
    for cc in range(2):
        score = lax.dot_general(flat[:, :256], qall[16 * cc : 16 * cc + 8].reshape(256, 256), nt, preferred_element_type=F32)
        score = score + lax.dot_general(flat[:, 256:], qall[16 * cc + 8 : 16 * cc + 16].reshape(256, 256), nt, preferred_element_type=F32)
        ssend[cc, 0] = score[:, :128]
        ssend[cc, 1] = score[:, 128:]

    def settle(k, carry):
        to = around(k)
        remote(ssend.at[to % 2, to // 8], sgot.at[k - 1], s_send, s_recv, plane(to))
        return carry

    lax.fori_loop(1, 16, settle, 0)
    wait(sgot, s_recv)
    total = ssend[u % 2, u // 8]
    for k in range(15):
        total = total + sgot[k]
    group = (u // 2) % 4
    result = jnp.zeros((4, 32), F32)
    for g in range(4):
        result = result + jnp.where(group == g, total[:4, 32 * g : 32 * g + 32], 0.0)
    out[...] = result

    for h in range(2):
        wait(got.at[h], rs_send.at[h])
        wait(zgot.at[h], z_send.at[h])
    wait(qall.at[0:15], q_send)
    wait(qall.at[0:16], c_send)
    wait(kgot.at[0:7], k_send)
    wait(sgot, s_send)


def on_device(acts, grads, proj_in, proj_out, queries, lengths, loss_mask):
    hbm = pl.BlockSpec(memory_space=pltpu.HBM)
    vmem = pl.BlockSpec(memory_space=pltpu.VMEM)
    smem = pl.BlockSpec(memory_space=pltpu.SMEM)
    dma = pltpu.SemaphoreType.DMA
    ff, dm = acts.shape[2], grads.shape[2]
    return pl.pallas_call(
        kernel,
        out_shape=jax.ShapeDtypeStruct((4, 32), F32),
        in_specs=[hbm, hbm, hbm, hbm, hbm, smem, vmem],
        out_specs=vmem,
        scratch_shapes=[
            pltpu.VMEM((8, 256, ff), BF16),
            pltpu.VMEM((8, 256, dm), BF16),
            pltpu.VMEM((2, ff, 64), BF16),
            pltpu.VMEM((2, dm, 64), BF16),
            pltpu.VMEM((16, 128, 128), F32),
            pltpu.VMEM((2, 15, 64, 128), F32),
            pltpu.VMEM((2, 64, 128), F32),
            pltpu.VMEM((2, 64, 128), F32),
            pltpu.VMEM((8, 8, 128), F32),
            pltpu.VMEM((8, 8, 128), F32),
            pltpu.VMEM((32, 32, 256), BF16),
            pltpu.VMEM((2, 2, 8, 128), F32),
            pltpu.VMEM((15, 8, 128), F32),
            dma((2, 8)), dma((2,)), dma,
            dma((2,)), dma((2,)), dma, dma, dma, dma,
            dma((2,)), dma((2,)), dma, dma, dma, dma,
        ],
        compiler_params=pltpu.CompilerParams(
            collective_id=0, has_side_effects=True, vmem_limit_bytes=32 << 20
        ),
        cost_estimate=pl.CostEstimate(flops=310_000_000, bytes_accessed=6_000_000, transcendentals=0),
        name="attribute",
    )(acts, grads, proj_in, proj_out, queries, lengths, loss_mask)


def solution(mesh):
    placed = (
        P(None, "dp", "tensor"),
        P(None, "dp", "tensor"),
        P(None, "tensor", None),
        P(None, "tensor", None),
        P("dp", "tensor"),
        P("dp"),
        P("dp", None),
    )
    return jax.shard_map(
        on_device, mesh=mesh, in_specs=placed, out_specs=P("dp", "tensor"), check_vma=False
    )
```

```python
import jax
import jax.numpy as jnp
from jax import lax
from jax.experimental import pallas as pl
from jax.experimental.pallas import tpu as pltpu
from jax.sharding import PartitionSpec as P

MESH = pl.DeviceIdType.MESH
F32 = jnp.float32
BF16 = jnp.bfloat16
AHEAD = 2


def kernel(acts, grads, pin, pout, qry, lens, mask, out,
           lensv, maskv, av, gv, piv, pov, part, gota, gotb, suma, sumb, fina, finb, zsum, zgot, ksend, kgot, qall, ssend, sgot,
           load_sem, w_sem, s_sem, own_sem, a_send, a_recv, b_send, b_recv, a2_send, a2_recv, b2_send, b2_recv, q_send, q_recv, c_send, c_recv,
           z_send, z_recv, k_send, k_recv, s_send, s_recv):
    nt = (((1,), (1,)), ((), ()))
    d = lax.axis_index("dp")
    t = lax.axis_index("tensor")
    zl, c = d // 2, d % 2
    u, zh = t // 2, t % 2
    x, y = u // 4, u % 4
    z = zh * 8 + zl

    def plane(index):
        return {"dp": d, "tensor": 2 * index + zh}

    def around(k):
        return ((x + k // 4) % 4) * 4 + (y + k % 4) % 4

    def column(k):
        zz = (z + k) % 16
        return {"dp": 2 * (zz % 8) + c, "tensor": 2 * u + zz // 8}

    sibling = {"dp": 2 * zl + 1 - c, "tensor": t}
    across = {"dp": d, "tensor": 2 * u + 1 - zh}

    def remote(src, dst, send, recv, where):
        pltpu.make_async_remote_copy(
            src_ref=src, dst_ref=dst, send_sem=send, recv_sem=recv, device_id=where, device_id_type=MESH
        ).start()

    def wait(ref, sem):
        pltpu.make_async_copy(ref, ref, sem).wait()

    def loads(i):
        layer, seq = i // 4, i % 4
        rows = pl.ds(pl.multiple_of(seq * 256, 256), 256)
        return (
            pltpu.make_async_copy(acts.at[layer, rows], av.at[i], load_sem.at[0, i]),
            pltpu.make_async_copy(grads.at[layer, rows], gv.at[i], load_sem.at[1, i]),
        )

    load_pin = pltpu.make_async_copy(pin, piv, w_sem.at[0])
    load_pout = pltpu.make_async_copy(pout, pov, w_sem.at[1])
    load_pin.start()
    load_pout.start()

    def start_load(i, carry):
        for copy in loads(i):
            copy.start()
        return carry

    lax.fori_loop(0, 8, start_load, 0)
    own_q = pltpu.make_async_copy(
        qry.at[pl.ds(pl.multiple_of(32 * zh, 32), 32)], qall.at[(2 * c + zh) * 8 + zl], own_sem
    )
    own_q.start()
    load_lens = pltpu.make_async_copy(lens, lensv, s_sem.at[0])
    load_mask = pltpu.make_async_copy(mask, maskv, s_sem.at[1])
    load_lens.start()
    load_mask.start()

    barrier = pltpu.get_barrier_semaphore()

    def greet(k, carry):
        pl.semaphore_signal(barrier, inc=1, device_id=column(k), device_id_type=MESH)
        pl.semaphore_signal(barrier, inc=1, device_id=plane(around(k)), device_id_type=MESH)
        return carry

    lax.fori_loop(1, 16, greet, 0)
    pl.semaphore_signal(barrier, inc=1, device_id=sibling, device_id_type=MESH)

    load_pin.wait()
    load_pout.wait()

    mine = u % 8
    yh, yl = y // 2, y % 2

    def project(xb, yb):
        i = 2 * xb + yb
        for copy in loads(i):
            copy.wait()
        layer = xb // 2
        inner = lax.dot_general(av[i], piv[layer], nt, preferred_element_type=F32)
        outer = lax.dot_general(gv[i], pov[layer], nt, preferred_element_type=F32)
        part[i, :, :, 0:64] = inner.reshape(4, 64, 64)
        part[i, :, :, 64:128] = outer.reshape(4, 64, 64)

    def place(q):
        r = q % 4
        step = jnp.where(r == 0, 2, jnp.where(r == 1, 1, jnp.where(r == 2, 3, 0)))
        return (x + step) % 4, jnp.where(q < 4, 1 - yh, yh)

    def give(xb, yb):
        i = 2 * xb + yb

        @pl.when(xb != x)
        def _():
            remote(part.at[i, 0:2], gota.at[x, pl.ds(2 * yb, 2)], a_send, a_recv.at[yb], plane(4 * xb + y))

        for sub in range(2):
            to = 2 * yb + sub

            @pl.when(to != y)
            def _():
                remote(part.at[i, 2 + sub], gotb.at[y, xb], b_send, b_recv.at[xb], plane(4 * x + to))

    def spread(k):
        far = (z + k) % 16 // 8
        remote(qry.at[pl.ds(pl.multiple_of(32 * far, 32), 32)], qall.at[(2 * c + zh) * 8 + zl], q_send, q_recv, column(k))

    def early(q, carry):
        project(*place(q))
        return carry

    lax.fori_loop(0, AHEAD, early, 0)
    pl.semaphore_wait(barrier, 31)

    def late(q, carry):
        give(*place(q))
        spread(2 * q + 1)
        spread(2 * q + 2)
        return carry

    lax.fori_loop(0, AHEAD, late, 0)

    def steady(q, carry):
        project(*place(q))
        give(*place(q))
        spread(2 * q + 1)

        @pl.when(q < 7)
        def _():
            spread(2 * q + 2)

        return carry

    lax.fori_loop(AHEAD, 8, steady, 0)

    def sum_a(yy):
        total = part[2 * x + yy // 2, yy % 2]
        for k in range(1, 4):
            total = total + gota[(x + k) % 4, yy]
        return total

    def sum_b(xx):
        total = part[2 * xx + yh, 2 + yl]
        for k in range(1, 4):
            total = total + gotb[(y + k) % 4, xx]
        return total

    def pass_a(yy):
        suma[yy] = sum_a(yy)
        remote(suma.at[yy], fina.at[y], a2_send, a2_recv, plane(4 * x + yy))

    def pass_b(xx):
        sumb[xx] = sum_b(xx)
        remote(sumb.at[xx], finb.at[x], b2_send, b2_recv, plane(4 * xx + y))

    wait(gota.at[0:3, 0:2], a_recv.at[1 - yh])
    pass_a(2 - 2 * yh)
    pass_a(3 - 2 * yh)
    for step in (2, 1, 3):
        xx = (x + step) % 4
        wait(gotb.at[0:3, 0], b_recv.at[xx])
        pass_b(xx)
    wait(gota.at[0:3, 0:2], a_recv.at[yh])
    pass_a(2 * yh + 1 - yl)
    total = sum_a(y)
    wait(fina.at[0:3], a2_recv)
    for k in range(1, 4):
        total = total + fina[(y + k) % 4]
    zsum[0] = total
    remote(zsum.at[0], zgot.at[0], z_send.at[0], z_recv.at[0], across)
    wait(gotb.at[0:3, 0], b_recv.at[x])
    total = sum_b(x)
    wait(finb.at[0:3], b2_recv)
    for k in range(1, 4):
        total = total + finb[(x + k) % 4]
    zsum[1] = total
    remote(zsum.at[1], zgot.at[1], z_send.at[1], z_recv.at[1], across)

    own_q.wait()
    wait(qall.at[0:15], q_recv)
    core_half = qall.at[pl.ds(16 * c, 16)]
    remote(core_half, core_half, c_send, c_recv, sibling)

    load_lens.wait()
    load_mask.wait()
    seq = (u // 2) % 4
    lane = lax.broadcasted_iota(jnp.int32, (128, 128), 1)
    lane4 = lane[:4]
    low4 = lane4 < 64
    first, second = maskv[:, :128], maskv[:, 128:]
    even = jnp.where(low4, first, pltpu.roll(second, 64, 1))
    odd = jnp.where(low4, pltpu.roll(first, 64, 1), second)
    marks = jnp.where(lax.broadcasted_iota(jnp.int32, (4, 128), 0) == seq, jnp.where(yl == 0, even, odd), 0)
    counted = jnp.sum(marks, axis=0, keepdims=True)
    slots = lane[:1] + 64 * yl + jnp.where(lane[:1] < 64, 0, 64)
    live = jnp.where(slots < lensv[seq], counted, 0).astype(F32)

    for h in range(2):
        wait(zgot.at[h], z_recv.at[h])
    unit = jnp.concatenate([zsum[0] + zgot[0], zsum[1] + zgot[1]], axis=0)
    weighted = unit.T[64:128] * live
    twice = jnp.where(lane < 64, unit, pltpu.roll(unit, 64, 1))
    wh, th = weighted.astype(BF16), twice.astype(BF16)
    wl, tl = (weighted - wh.astype(F32)).astype(BF16), (twice - th.astype(F32)).astype(BF16)
    kron = jnp.dot(
        jnp.concatenate([wh, wh, wl], axis=1), jnp.concatenate([th, tl, th], axis=0), preferred_element_type=F32
    )
    ksend[...] = kron.reshape(8, 8, 128)
    def hand(k, carry):
        to = (mine + k) % 8
        remote(ksend.at[to], kgot.at[mine], k_send, k_recv, plane((u // 8) * 8 + to))
        return carry

    lax.fori_loop(1, 8, hand, 0)
    kgot[mine] = ksend[mine]
    wait(qall.at[0:16], c_recv)
    wait(kgot.at[0:7], k_recv)
    rows8 = []
    for s in range(4):
        rows8.append(kgot[2 * s] + kgot[2 * s + 1])
    stacked = jnp.stack(rows8, axis=0)
    low = lax.broadcasted_iota(jnp.int32, (4, 128), 1) < 64
    flat = jnp.concatenate(
        [jnp.where(low, stacked[:, 2 * r, :], stacked[:, 2 * r + 1, :]) for r in range(4)], axis=1
    )
    flat = jnp.concatenate([flat, jnp.zeros_like(flat)], axis=0).astype(BF16)
    for cc in range(2):
        score = lax.dot_general(flat[:, :256], qall[16 * cc : 16 * cc + 8].reshape(256, 256), nt, preferred_element_type=F32)
        score = score + lax.dot_general(flat[:, 256:], qall[16 * cc + 8 : 16 * cc + 16].reshape(256, 256), nt, preferred_element_type=F32)
        ssend[cc, 0] = score[:, :128]
        ssend[cc, 1] = score[:, 128:]

    def settle(k, carry):
        to = around(k)
        remote(ssend.at[to % 2, to // 8], sgot.at[k - 1], s_send, s_recv, plane(to))
        return carry

    lax.fori_loop(1, 16, settle, 0)
    wait(sgot, s_recv)
    total = ssend[u % 2, u // 8]
    for k in range(15):
        total = total + sgot[k]
    group = (u // 2) % 4
    result = jnp.zeros((4, 32), F32)
    for g in range(4):
        result = result + jnp.where(group == g, total[:4, 32 * g : 32 * g + 32], 0.0)
    out[...] = result

    for h in range(2):
        wait(zgot.at[h], z_send.at[h])
    wait(gota.at[0:3], a_send)
    wait(gotb.at[0:3], b_send)
    wait(fina.at[0:3], a2_send)
    wait(finb.at[0:3], b2_send)
    wait(qall.at[0:15], q_send)
    wait(qall.at[0:16], c_send)
    wait(kgot.at[0:7], k_send)
    wait(sgot, s_send)


def on_device(acts, grads, proj_in, proj_out, queries, lengths, loss_mask):
    hbm = pl.BlockSpec(memory_space=pltpu.HBM)
    vmem = pl.BlockSpec(memory_space=pltpu.VMEM)
    dma = pltpu.SemaphoreType.DMA
    ff, dm = acts.shape[2], grads.shape[2]
    return pl.pallas_call(
        kernel,
        out_shape=jax.ShapeDtypeStruct((4, 32), F32),
        in_specs=[hbm] * 7,
        out_specs=vmem,
        scratch_shapes=[
            pltpu.SMEM((4,), jnp.int32),
            pltpu.VMEM((4, 256), jnp.int32),
            pltpu.VMEM((8, 256, ff), BF16),
            pltpu.VMEM((8, 256, dm), BF16),
            pltpu.VMEM((2, 64, ff), BF16),
            pltpu.VMEM((2, 64, dm), BF16),
            pltpu.VMEM((8, 4, 64, 128), F32),
            pltpu.VMEM((4, 4, 64, 128), F32),
            pltpu.VMEM((4, 4, 64, 128), F32),
            pltpu.VMEM((4, 64, 128), F32),
            pltpu.VMEM((4, 64, 128), F32),
            pltpu.VMEM((4, 64, 128), F32),
            pltpu.VMEM((4, 64, 128), F32),
            pltpu.VMEM((2, 64, 128), F32),
            pltpu.VMEM((2, 64, 128), F32),
            pltpu.VMEM((8, 8, 128), F32),
            pltpu.VMEM((8, 8, 128), F32),
            pltpu.VMEM((32, 32, 256), BF16),
            pltpu.VMEM((2, 2, 8, 128), F32),
            pltpu.VMEM((15, 8, 128), F32),
            dma((2, 8)), dma((2,)), dma((2,)), dma,
            dma, dma((2,)), dma, dma((4,)), dma, dma, dma, dma, dma, dma, dma, dma,
            dma((2,)), dma((2,)), dma, dma, dma, dma,
        ],
        compiler_params=pltpu.CompilerParams(
            collective_id=0, has_side_effects=True, vmem_limit_bytes=60 << 20
        ),
        cost_estimate=pl.CostEstimate(flops=310_000_000, bytes_accessed=6_000_000, transcendentals=0),
        name="attribute",
    )(acts, grads, proj_in.transpose(0, 2, 1), proj_out.transpose(0, 2, 1), queries, lengths, loss_mask)


def solution(mesh):
    placed = (
        P(None, "dp", "tensor"),
        P(None, "dp", "tensor"),
        P(None, "tensor", None),
        P(None, "tensor", None),
        P("dp", "tensor"),
        P("dp"),
        P("dp", None),
    )
    return jax.shard_map(
        on_device, mesh=mesh, in_specs=placed, out_specs=P("dp", "tensor"), check_vma=False
    )
```

```python
import jax
import jax.numpy as jnp
from jax import lax
from jax.experimental import pallas as pl
from jax.experimental.pallas import tpu as pltpu
from jax.sharding import PartitionSpec as P

MESH = pl.DeviceIdType.MESH
F32 = jnp.float32
BF16 = jnp.bfloat16
AHEAD = 2


def kernel(acts, grads, pin, pout, qry, lens, mask, out,
           lensv, maskv, av, gv, piv, pov, part, gota, gotb, suma, sumb, fina, finb, zsum, zgot, ksend, kgot, qall, ssend, sgot,
           load_sem, w_sem, s_sem, own_sem, a_send, a_recv, b_send, b_recv, a2_send, a2_recv, b2_send, b2_recv, q_send, q_recv, p_send, p_recv, c_send, c_recv,
           z_send, z_recv, k_send, k_recv, s_send, s_recv, across_in, later_in):
    nt = (((1,), (1,)), ((), ()))
    d = lax.axis_index("dp")
    t = lax.axis_index("tensor")
    zl, c = d // 2, d % 2
    u, zh = t // 2, t % 2
    x, y = u // 4, u % 4
    low = zl % 2
    z = zh * 8 + zl

    def plane(index):
        return {"dp": d, "tensor": 2 * index + zh}

    def around(k):
        return ((x + k // 4) % 4) * 4 + (y + k % 4) % 4

    def column(k):
        zz = (z + k) % 16
        return {"dp": 2 * (zz % 8) + c, "tensor": 2 * u + zz // 8}

    beside = {"dp": 2 * (zl + 1 - 2 * low) + c, "tensor": t}
    sibling = {"dp": 2 * zl + 1 - c, "tensor": t}
    across = {"dp": d, "tensor": 2 * u + 1 - zh}

    def remote(src, dst, send, recv, where):
        pltpu.make_async_remote_copy(
            src_ref=src, dst_ref=dst, send_sem=send, recv_sem=recv, device_id=where, device_id_type=MESH
        ).start()

    def wait(ref, sem):
        pltpu.make_async_copy(ref, ref, sem).wait()

    def loads(i):
        layer, seq = i // 4, i % 4
        rows = pl.ds(pl.multiple_of(seq * 256, 256), 256)
        return (
            pltpu.make_async_copy(acts.at[layer, rows], av.at[i], load_sem.at[0, i]),
            pltpu.make_async_copy(grads.at[layer, rows], gv.at[i], load_sem.at[1, i]),
        )

    load_pin = pltpu.make_async_copy(pin, piv, w_sem.at[0])
    load_pout = pltpu.make_async_copy(pout, pov, w_sem.at[1])
    load_pin.start()
    load_pout.start()

    def start_load(i, carry):
        for copy in loads(i):
            copy.start()
        return carry

    lax.fori_loop(0, 8, start_load, 0)
    slot = ((2 * c + low) * 2 + zh) * 4 + zl // 2
    own_q = pltpu.make_async_copy(
        qry.at[pl.ds(pl.multiple_of(32 * zh, 32), 32)], qall.at[slot], own_sem
    )
    own_q.start()
    load_lens = pltpu.make_async_copy(lens, lensv, s_sem.at[0])
    load_mask = pltpu.make_async_copy(mask, maskv, s_sem.at[1])
    load_lens.start()
    load_mask.start()

    barrier = pltpu.get_barrier_semaphore()

    def greet(where):
        pl.semaphore_signal(barrier, inc=1, device_id=where, device_id_type=MESH)

    for k in (1, 2, 3, 4, 8, 12):
        greet(plane(around(k)))
    for k in range(1, 8):

        @pl.when((z + 2 * k) % 16 > z)
        def _():
            greet(column(2 * k))

    @pl.when(low == 0)
    def _():
        greet(beside)

    @pl.when(c == 0)
    def _():
        greet(sibling)

    load_pin.wait()
    load_pout.wait()

    mine = u % 8
    yh, yl = y // 2, y % 2

    def project(xb, yb):
        i = 2 * xb + yb
        for copy in loads(i):
            copy.wait()
        layer = xb // 2
        inner = lax.dot_general(av[i], piv[layer], nt, preferred_element_type=F32)
        outer = lax.dot_general(gv[i], pov[layer], nt, preferred_element_type=F32)
        part[i, :, :, 0:64] = inner.reshape(4, 64, 64)
        part[i, :, :, 64:128] = outer.reshape(4, 64, 64)

    def place(q):
        r = q % 4
        step = jnp.where(r == 0, 2, jnp.where(r == 1, 1, jnp.where(r == 2, 3, 0)))
        return (x + step) % 4, jnp.where(q < 4, 1 - yh, yh)

    def give(xb, yb):
        i = 2 * xb + yb

        @pl.when(xb != x)
        def _():
            remote(part.at[i, 0:2], gota.at[x, pl.ds(2 * yb, 2)], a_send, a_recv.at[yb], plane(4 * xb + y))

        for sub in range(2):
            to = 2 * yb + sub

            @pl.when(to != y)
            def _():
                remote(part.at[i, 2 + sub], gotb.at[y, xb], b_send, b_recv.at[xb], plane(4 * x + to))

    def early(q, carry):
        project(*place(q))
        return carry

    lax.fori_loop(0, AHEAD, early, 0)
    pl.semaphore_wait(barrier, 6 + z // 2 + low + c)

    def answer(where, sem):
        pl.semaphore_signal(sem, inc=1, device_id=where, device_id_type=MESH)

    def spread(k):
        far = (z + 2 * k) % 16 // 8
        remote(qry.at[pl.ds(pl.multiple_of(32 * far, 32), 32)], qall.at[slot], q_send, q_recv, column(2 * k))

    @pl.when(z >= 8)
    def _():
        answer(across, across_in)

    for k in range(1, 8):

        @pl.when((z + 2 * k) % 16 < z)
        def _():
            answer(column(2 * k), later_in)
            spread(k)

    @pl.when(low == 1)
    def _():
        answer(beside, later_in)

    @pl.when(c == 1)
    def _():
        answer(sibling, later_in)


    def late(q, carry):
        give(*place(q))
        return carry

    lax.fori_loop(0, AHEAD, late, 0)

    def steady(q, carry):
        project(*place(q))
        give(*place(q))
        return carry

    lax.fori_loop(AHEAD, 8, steady, 0)

    def sum_a(yy):
        total = part[2 * x + yy // 2, yy % 2]
        for k in range(1, 4):
            total = total + gota[(x + k) % 4, yy]
        return total

    def sum_b(xx):
        total = part[2 * xx + yh, 2 + yl]
        for k in range(1, 4):
            total = total + gotb[(y + k) % 4, xx]
        return total

    def pass_a(yy):
        suma[yy] = sum_a(yy)
        remote(suma.at[yy], fina.at[y], a2_send, a2_recv, plane(4 * x + yy))

    def pass_b(xx):
        sumb[xx] = sum_b(xx)
        remote(sumb.at[xx], finb.at[x], b2_send, b2_recv, plane(4 * xx + y))

    later = 9 - z // 2 - low - c

    @pl.when(later > 0)
    def _():
        pl.semaphore_wait(later_in, later)

    for k in range(1, 8):

        @pl.when((z + 2 * k) % 16 > z)
        def _():
            spread(k)

    wait(gota.at[0:3, 0:2], a_recv.at[1 - yh])
    pass_a(2 - 2 * yh)
    pass_a(3 - 2 * yh)
    for step in (2, 1, 3):
        xx = (x + step) % 4
        wait(gotb.at[0:3, 0], b_recv.at[xx])
        pass_b(xx)
    wait(gota.at[0:3, 0:2], a_recv.at[yh])
    pass_a(2 * yh + 1 - yl)
    total = sum_a(y)
    wait(fina.at[0:3], a2_recv)
    for k in range(1, 4):
        total = total + fina[(y + k) % 4]
    zsum[0] = total

    @pl.when(z < 8)
    def _():
        pl.semaphore_wait(across_in, 1)

    remote(zsum.at[0], zgot.at[0], z_send.at[0], z_recv.at[0], across)
    wait(gotb.at[0:3, 0], b_recv.at[x])
    total = sum_b(x)
    wait(finb.at[0:3], b2_recv)
    for k in range(1, 4):
        total = total + finb[(x + k) % 4]
    zsum[1] = total
    remote(zsum.at[1], zgot.at[1], z_send.at[1], z_recv.at[1], across)

    own_q.wait()
    wait(qall.at[0:7], q_recv)
    column_half = qall.at[pl.ds(16 * c + 8 * low, 8)]
    remote(column_half, column_half, p_send, p_recv, beside)

    load_lens.wait()
    load_mask.wait()
    seq = (u // 2) % 4
    lane = lax.broadcasted_iota(jnp.int32, (128, 128), 1)
    lane4 = lane[:4]
    low4 = lane4 < 64
    first, second = maskv[:, :128], maskv[:, 128:]
    even = jnp.where(low4, first, pltpu.roll(second, 64, 1))
    odd = jnp.where(low4, pltpu.roll(first, 64, 1), second)
    marks = jnp.where(lax.broadcasted_iota(jnp.int32, (4, 128), 0) == seq, jnp.where(yl == 0, even, odd), 0)
    counted = jnp.sum(marks, axis=0, keepdims=True)
    slots = lane[:1] + 64 * yl + jnp.where(lane[:1] < 64, 0, 64)
    live = jnp.where(slots < lensv[seq], counted, 0).astype(F32)

    for h in range(2):
        wait(zgot.at[h], z_recv.at[h])
    wait(qall.at[0:8], p_recv)
    core_half = qall.at[pl.ds(16 * c, 16)]
    remote(core_half, core_half, c_send, c_recv, sibling)
    unit = jnp.concatenate([zsum[0] + zgot[0], zsum[1] + zgot[1]], axis=0)
    weighted = unit.T[64:128] * live
    twice = jnp.where(lane < 64, unit, pltpu.roll(unit, 64, 1))
    wh, th = weighted.astype(BF16), twice.astype(BF16)
    wl, tl = (weighted - wh.astype(F32)).astype(BF16), (twice - th.astype(F32)).astype(BF16)
    kron = jnp.dot(
        jnp.concatenate([wh, wh, wl], axis=1), jnp.concatenate([th, tl, th], axis=0), preferred_element_type=F32
    )
    ksend[...] = kron.reshape(8, 8, 128)
    for k in range(1, 8):
        to = (mine + k) % 8
        remote(ksend.at[to], kgot.at[mine], k_send, k_recv, plane((u // 8) * 8 + to))
    kgot[mine] = ksend[mine]
    wait(qall.at[0:16], c_recv)
    wait(kgot.at[0:7], k_recv)
    rows8 = []
    for s in range(4):
        rows8.append(kgot[2 * s] + kgot[2 * s + 1])
    stacked = jnp.stack(rows8, axis=0)
    flat = jnp.concatenate(
        [jnp.where(low4, stacked[:, 2 * r, :], stacked[:, 2 * r + 1, :]) for r in range(4)], axis=1
    )
    flat = jnp.concatenate([flat, jnp.zeros_like(flat)], axis=0).astype(BF16)
    for m in range(4):
        ssend[m] = sum(
            lax.dot_general(
                flat[:, 256 * e : 256 * e + 256], qall[8 * m + 4 * e : 8 * m + 4 * e + 4].reshape(128, 256), nt,
                preferred_element_type=F32,
            )
            for e in range(2)
        )
    for k in range(1, 16):
        to = around(k)
        remote(ssend.at[to % 2 * 2 + to // 2 % 2], sgot.at[k - 1], s_send, s_recv, plane(to))
    wait(sgot, s_recv)
    total = ssend[u % 2 * 2 + u // 2 % 2]
    for k in range(15):
        total = total + sgot[k]
    result = jnp.zeros((4, 32), F32)
    for g in range(4):
        result = result + jnp.where(x == g, total[:4, 32 * g : 32 * g + 32], 0.0)
    out[...] = result

    for h in range(2):
        wait(zgot.at[h], z_send.at[h])
    wait(gota.at[0:3], a_send)
    wait(gotb.at[0:3], b_send)
    wait(fina.at[0:3], a2_send)
    wait(finb.at[0:3], b2_send)
    wait(qall.at[0:7], q_send)
    wait(qall.at[0:8], p_send)
    wait(qall.at[0:16], c_send)
    wait(kgot.at[0:7], k_send)
    wait(sgot, s_send)


def on_device(acts, grads, proj_in, proj_out, queries, lengths, loss_mask):
    hbm = pl.BlockSpec(memory_space=pltpu.HBM)
    vmem = pl.BlockSpec(memory_space=pltpu.VMEM)
    dma = pltpu.SemaphoreType.DMA
    ff, dm = acts.shape[2], grads.shape[2]
    return pl.pallas_call(
        kernel,
        out_shape=jax.ShapeDtypeStruct((4, 32), F32),
        in_specs=[hbm] * 7,
        out_specs=vmem,
        scratch_shapes=[
            pltpu.SMEM((4,), jnp.int32),
            pltpu.VMEM((4, 256), jnp.int32),
            pltpu.VMEM((8, 256, ff), BF16),
            pltpu.VMEM((8, 256, dm), BF16),
            pltpu.VMEM((2, 64, ff), BF16),
            pltpu.VMEM((2, 64, dm), BF16),
            pltpu.VMEM((8, 4, 64, 128), F32),
            pltpu.VMEM((4, 4, 64, 128), F32),
            pltpu.VMEM((4, 4, 64, 128), F32),
            pltpu.VMEM((4, 64, 128), F32),
            pltpu.VMEM((4, 64, 128), F32),
            pltpu.VMEM((4, 64, 128), F32),
            pltpu.VMEM((4, 64, 128), F32),
            pltpu.VMEM((2, 64, 128), F32),
            pltpu.VMEM((2, 64, 128), F32),
            pltpu.VMEM((8, 8, 128), F32),
            pltpu.VMEM((8, 8, 128), F32),
            pltpu.VMEM((32, 32, 256), BF16),
            pltpu.VMEM((4, 8, 128), F32),
            pltpu.VMEM((15, 8, 128), F32),
            dma((2, 8)), dma((2,)), dma((2,)), dma,
            dma, dma((2,)), dma, dma((4,)), dma, dma, dma, dma, dma, dma, dma, dma, dma, dma,
            dma((2,)), dma((2,)), dma, dma, dma, dma,
            pltpu.SemaphoreType.REGULAR, pltpu.SemaphoreType.REGULAR,
        ],
        compiler_params=pltpu.CompilerParams(
            collective_id=0, has_side_effects=True, vmem_limit_bytes=60 << 20
        ),
        cost_estimate=pl.CostEstimate(flops=310_000_000, bytes_accessed=6_000_000, transcendentals=0),
        name="attribute",
    )(acts, grads, proj_in.transpose(0, 2, 1), proj_out.transpose(0, 2, 1), queries, lengths, loss_mask)


def solution(mesh):
    placed = (
        P(None, "dp", "tensor"),
        P(None, "dp", "tensor"),
        P(None, "tensor", None),
        P(None, "tensor", None),
        P("dp", "tensor"),
        P("dp"),
        P("dp", None),
    )
    return jax.shard_map(
        on_device, mesh=mesh, in_specs=placed, out_specs=P("dp", "tensor"), check_vma=False
    )
```

```python
import jax
import jax.numpy as jnp
from jax import lax
from jax.experimental import pallas as pl
from jax.experimental.pallas import tpu as pltpu
from jax.sharding import PartitionSpec as P

MESH = pl.DeviceIdType.MESH
F32 = jnp.float32
BF16 = jnp.bfloat16
AHEAD = 2
FAR_FIRST = sorted(range(1, 16), key=lambda k: -min(k // 4, 4 - k // 4) - min(k % 4, 4 - k % 4))


def kernel(acts, grads, pin, pout, qry, lens, mask, out,
           lensv, maskv, av, gv, piv, pov, part, gota, gotb, suma, sumb, fina, finb, zsum, zgot, ksend, kgot, qall, ssend, sgot,
           load_sem, w_sem, s_sem, own_sem, a_send, a_recv, b_send, b_recv, a2_send, a2_recv, b2_send, b2_recv, q_send, q_recv, p_send, p_recv, c_send, c_recv,
           z_send, z_recv, k_send, k_recv, s_send, s_recv, across_in, later_in):
    nt = (((1,), (1,)), ((), ()))
    d = lax.axis_index("dp")
    t = lax.axis_index("tensor")
    zl, c = d // 2, d % 2
    u, zh = t // 2, t % 2
    x, y = u // 4, u % 4
    low = zl % 2
    z = zh * 8 + zl

    def plane(index):
        return {"dp": d, "tensor": 2 * index + zh}

    def around(k):
        return ((x + k // 4) % 4) * 4 + (y + k % 4) % 4

    def column(k):
        zz = (z + k) % 16
        return {"dp": 2 * (zz % 8) + c, "tensor": 2 * u + zz // 8}

    beside = {"dp": 2 * (zl + 1 - 2 * low) + c, "tensor": t}
    sibling = {"dp": 2 * zl + 1 - c, "tensor": t}
    across = {"dp": d, "tensor": 2 * u + 1 - zh}

    def remote(src, dst, send, recv, where):
        pltpu.make_async_remote_copy(
            src_ref=src, dst_ref=dst, send_sem=send, recv_sem=recv, device_id=where, device_id_type=MESH
        ).start()

    def wait(ref, sem):
        pltpu.make_async_copy(ref, ref, sem).wait()

    def loads(i):
        layer, seq = i // 4, i % 4
        rows = pl.ds(pl.multiple_of(seq * 256, 256), 256)
        return (
            pltpu.make_async_copy(acts.at[layer, rows], av.at[i], load_sem.at[0, i]),
            pltpu.make_async_copy(grads.at[layer, rows], gv.at[i], load_sem.at[1, i]),
        )

    barrier = pltpu.get_barrier_semaphore()

    def greet(where):
        pl.semaphore_signal(barrier, inc=1, device_id=where, device_id_type=MESH)

    for k in (1, 2, 3, 4, 8, 12):
        greet(plane(around(k)))

    load_pin = pltpu.make_async_copy(pin, piv, w_sem.at[0])
    load_pout = pltpu.make_async_copy(pout, pov, w_sem.at[1])
    load_pin.start()
    load_pout.start()

    yh, yl = y // 2, y % 2

    def place(q):
        r = q % 4
        step = jnp.where(r == 0, 2, jnp.where(r == 1, 1, jnp.where(r == 2, 3, 0)))
        return (x + step) % 4, jnp.where(q < 4, 1 - yh, yh)

    def start_load(q, carry):
        xb, yb = place(q)
        for copy in loads(2 * xb + yb):
            copy.start()
        return carry

    lax.fori_loop(0, 8, start_load, 0)
    slot = ((2 * c + low) * 2 + zh) * 4 + zl // 2
    own_q = pltpu.make_async_copy(
        qry.at[pl.ds(pl.multiple_of(32 * zh, 32), 32)], qall.at[slot], own_sem
    )
    own_q.start()
    load_lens = pltpu.make_async_copy(lens, lensv, s_sem.at[0])
    load_mask = pltpu.make_async_copy(mask, maskv, s_sem.at[1])
    load_lens.start()
    load_mask.start()

    for k in range(1, 8):

        @pl.when((z + 2 * k) % 16 > z)
        def _():
            greet(column(2 * k))

    @pl.when(low == 0)
    def _():
        greet(beside)

    @pl.when(c == 0)
    def _():
        greet(sibling)

    load_pin.wait()
    load_pout.wait()

    mine = u % 8

    def project(xb, yb):
        i = 2 * xb + yb
        for copy in loads(i):
            copy.wait()
        layer = xb // 2
        inner = lax.dot_general(av[i], piv[layer], nt, preferred_element_type=F32)
        outer = lax.dot_general(gv[i], pov[layer], nt, preferred_element_type=F32)
        part[i, :, :, 0:64] = inner.reshape(4, 64, 64)
        part[i, :, :, 64:128] = outer.reshape(4, 64, 64)

    def give(xb, yb):
        i = 2 * xb + yb

        @pl.when(xb != x)
        def _():
            remote(part.at[i, 0:2], gota.at[x, pl.ds(2 * yb, 2)], a_send, a_recv.at[yb], plane(4 * xb + y))

        for sub in range(2):
            to = 2 * yb + sub

            @pl.when(to != y)
            def _():
                remote(part.at[i, 2 + sub], gotb.at[y, xb], b_send, b_recv.at[xb], plane(4 * x + to))

    def early(q, carry):
        project(*place(q))
        return carry

    lax.fori_loop(0, AHEAD, early, 0)
    pl.semaphore_wait(barrier, 6 + z // 2 + low + c)

    def answer(where, sem):
        pl.semaphore_signal(sem, inc=1, device_id=where, device_id_type=MESH)

    def spread(k):
        far = (z + 2 * k) % 16 // 8
        remote(qry.at[pl.ds(pl.multiple_of(32 * far, 32), 32)], qall.at[slot], q_send, q_recv, column(2 * k))

    @pl.when(z >= 8)
    def _():
        answer(across, across_in)

    for k in range(1, 8):

        @pl.when((z + 2 * k) % 16 < z)
        def _():
            answer(column(2 * k), later_in)
            spread(k)

    @pl.when(low == 1)
    def _():
        answer(beside, later_in)

    @pl.when(c == 1)
    def _():
        answer(sibling, later_in)


    def late(q, carry):
        give(*place(q))
        return carry

    lax.fori_loop(0, AHEAD, late, 0)

    def steady(q, carry):
        project(*place(q))
        give(*place(q))
        return carry

    lax.fori_loop(AHEAD, 8, steady, 0)

    def sum_a(yy):
        total = part[2 * x + yy // 2, yy % 2]
        for k in range(1, 4):
            total = total + gota[(x + k) % 4, yy]
        return total

    def sum_b(xx):
        total = part[2 * xx + yh, 2 + yl]
        for k in range(1, 4):
            total = total + gotb[(y + k) % 4, xx]
        return total

    def pass_a(yy):
        suma[yy] = sum_a(yy)
        remote(suma.at[yy], fina.at[y], a2_send, a2_recv, plane(4 * x + yy))

    def pass_b(xx):
        sumb[xx] = sum_b(xx)
        remote(sumb.at[xx], finb.at[x], b2_send, b2_recv, plane(4 * xx + y))

    later = 9 - z // 2 - low - c

    def meet():
        @pl.when(later > 0)
        def _():
            pl.semaphore_wait(later_in, later)

        for k in range(1, 8):

            @pl.when((z + 2 * k) % 16 > z)
            def _():
                spread(k)

    @pl.when(z >= 4)
    def _():
        meet()

    wait(gota.at[0:3, 0:2], a_recv.at[1 - yh])
    pass_a(2 - 2 * yh)
    pass_a(3 - 2 * yh)
    for step in (2, 1, 3):
        xx = (x + step) % 4
        wait(gotb.at[0:3, 0], b_recv.at[xx])
        pass_b(xx)
    wait(gota.at[0:3, 0:2], a_recv.at[yh])
    pass_a(2 * yh + 1 - yl)

    @pl.when(z < 4)
    def _():
        meet()

    total = sum_a(y)
    wait(fina.at[0:3], a2_recv)
    for k in range(1, 4):
        total = total + fina[(y + k) % 4]
    zsum[0] = total

    @pl.when(z < 8)
    def _():
        pl.semaphore_wait(across_in, 1)

    remote(zsum.at[0], zgot.at[0], z_send.at[0], z_recv.at[0], across)
    wait(gotb.at[0:3, 0], b_recv.at[x])
    total = sum_b(x)
    wait(finb.at[0:3], b2_recv)
    for k in range(1, 4):
        total = total + finb[(x + k) % 4]
    zsum[1] = total
    remote(zsum.at[1], zgot.at[1], z_send.at[1], z_recv.at[1], across)

    own_q.wait()
    wait(qall.at[0:7], q_recv)
    column_half = qall.at[pl.ds(16 * c + 8 * low, 8)]
    remote(column_half, column_half, p_send, p_recv, beside)
    remote(column_half, column_half, c_send.at[0], c_recv.at[0], sibling)

    load_lens.wait()
    load_mask.wait()
    seq = (u // 2) % 4
    lane = lax.broadcasted_iota(jnp.int32, (128, 128), 1)
    lane4 = lane[:4]
    low4 = lane4 < 64
    first, second = maskv[:, :128], maskv[:, 128:]
    even = jnp.where(low4, first, pltpu.roll(second, 64, 1))
    odd = jnp.where(low4, pltpu.roll(first, 64, 1), second)
    marks = jnp.where(lax.broadcasted_iota(jnp.int32, (4, 128), 0) == seq, jnp.where(yl == 0, even, odd), 0)
    counted = jnp.sum(marks, axis=0, keepdims=True)
    slots = lane[:1] + 64 * yl + jnp.where(lane[:1] < 64, 0, 64)
    live = jnp.where(slots < lensv[seq], counted, 0).astype(F32)

    def part_kron(h):
        unit = zsum[h] + zgot[h]
        weighted = unit.T[64:128] * live[:, 64 * h : 64 * h + 64]
        twice = jnp.where(lane[:64] < 64, unit, pltpu.roll(unit, 64, 1))
        wh, th = weighted.astype(BF16), twice.astype(BF16)
        wl, tl = (weighted - wh.astype(F32)).astype(BF16), (twice - th.astype(F32)).astype(BF16)
        return (
            jnp.dot(wh, th, preferred_element_type=F32)
            + jnp.dot(wh, tl, preferred_element_type=F32)
            + jnp.dot(wl, th, preferred_element_type=F32)
        )

    wait(gota.at[0:3], a_send)
    wait(gotb.at[0:3], b_send)
    wait(fina.at[0:3], a2_send)
    wait(finb.at[0:3], b2_send)
    wait(qall.at[0:7], q_send)
    wait(zgot.at[0], z_recv.at[0])
    kron = part_kron(0)
    wait(zgot.at[1], z_recv.at[1])
    kron = kron + part_kron(1)
    ksend[...] = kron.reshape(8, 8, 128)
    for k in range(1, 8):
        to = (mine + k) % 8
        remote(ksend.at[to], kgot.at[mine], k_send, k_recv, plane((u // 8) * 8 + to))
    kgot[mine] = ksend[mine]
    wait(qall.at[0:8], p_recv)
    other_half = qall.at[pl.ds(16 * c + 8 - 8 * low, 8)]
    remote(other_half, other_half, c_send.at[1], c_recv.at[1], sibling)
    wait(kgot.at[0:7], k_recv)
    for h in range(2):
        wait(qall.at[0:8], c_recv.at[h])
    rows8 = []
    for s in range(4):
        rows8.append(kgot[2 * s] + kgot[2 * s + 1])
    stacked = jnp.stack(rows8, axis=0)
    flat = jnp.concatenate(
        [jnp.where(low4, stacked[:, 2 * r, :], stacked[:, 2 * r + 1, :]) for r in range(4)], axis=1
    )
    flat = jnp.concatenate([flat, jnp.zeros_like(flat)], axis=0).astype(BF16)
    for m in range(4):
        ssend[m] = sum(
            lax.dot_general(
                flat[:, 256 * e : 256 * e + 256], qall[8 * m + 4 * e : 8 * m + 4 * e + 4].reshape(128, 256), nt,
                preferred_element_type=F32,
            )
            for e in range(2)
        )
    for k in FAR_FIRST:
        to = around(k)
        remote(ssend.at[to % 2 * 2 + to // 2 % 2], sgot.at[k - 1], s_send, s_recv, plane(to))
    for h in range(2):
        wait(zgot.at[h], z_send.at[h])
    wait(qall.at[0:8], p_send)
    for h in range(2):
        wait(qall.at[0:8], c_send.at[h])
    wait(kgot.at[0:7], k_send)
    wait(sgot, s_recv)
    total = ssend[u % 2 * 2 + u // 2 % 2]
    for k in range(15):
        total = total + sgot[k]
    result = jnp.zeros((4, 32), F32)
    for g in range(4):
        result = result + jnp.where(x == g, total[:4, 32 * g : 32 * g + 32], 0.0)
    out[...] = result
    wait(sgot, s_send)


def on_device(acts, grads, proj_in, proj_out, queries, lengths, loss_mask):
    hbm = pl.BlockSpec(memory_space=pltpu.HBM)
    vmem = pl.BlockSpec(memory_space=pltpu.VMEM)
    dma = pltpu.SemaphoreType.DMA
    ff, dm = acts.shape[2], grads.shape[2]
    return pl.pallas_call(
        kernel,
        out_shape=jax.ShapeDtypeStruct((4, 32), F32),
        in_specs=[hbm] * 7,
        out_specs=vmem,
        scratch_shapes=[
            pltpu.SMEM((4,), jnp.int32),
            pltpu.VMEM((4, 256), jnp.int32),
            pltpu.VMEM((8, 256, ff), BF16),
            pltpu.VMEM((8, 256, dm), BF16),
            pltpu.VMEM((2, 64, ff), BF16),
            pltpu.VMEM((2, 64, dm), BF16),
            pltpu.VMEM((8, 4, 64, 128), F32),
            pltpu.VMEM((4, 4, 64, 128), F32),
            pltpu.VMEM((4, 4, 64, 128), F32),
            pltpu.VMEM((4, 64, 128), F32),
            pltpu.VMEM((4, 64, 128), F32),
            pltpu.VMEM((4, 64, 128), F32),
            pltpu.VMEM((4, 64, 128), F32),
            pltpu.VMEM((2, 64, 128), F32),
            pltpu.VMEM((2, 64, 128), F32),
            pltpu.VMEM((8, 8, 128), F32),
            pltpu.VMEM((8, 8, 128), F32),
            pltpu.VMEM((32, 32, 256), BF16),
            pltpu.VMEM((4, 8, 128), F32),
            pltpu.VMEM((15, 8, 128), F32),
            dma((2, 8)), dma((2,)), dma((2,)), dma,
            dma, dma((2,)), dma, dma((4,)), dma, dma, dma, dma, dma, dma, dma, dma, dma((2,)), dma((2,)),
            dma((2,)), dma((2,)), dma, dma, dma, dma,
            pltpu.SemaphoreType.REGULAR, pltpu.SemaphoreType.REGULAR,
        ],
        compiler_params=pltpu.CompilerParams(
            collective_id=0, has_side_effects=True, vmem_limit_bytes=60 << 20
        ),
        cost_estimate=pl.CostEstimate(flops=310_000_000, bytes_accessed=6_000_000, transcendentals=0),
        name="attribute",
    )(acts, grads, proj_in.transpose(0, 2, 1), proj_out.transpose(0, 2, 1), queries, lengths, loss_mask)


def solution(mesh):
    placed = (
        P(None, "dp", "tensor"),
        P(None, "dp", "tensor"),
        P(None, "tensor", None),
        P(None, "tensor", None),
        P("dp", "tensor"),
        P("dp"),
        P("dp", None),
    )
    return jax.shard_map(
        on_device, mesh=mesh, in_specs=placed, out_specs=P("dp", "tensor"), check_vma=False
    )
```

```python
import jax
import jax.numpy as jnp
from jax import lax
from jax.experimental import pallas as pl
from jax.experimental.pallas import tpu as pltpu
from jax.sharding import PartitionSpec as P

MESH = pl.DeviceIdType.MESH
F32 = jnp.float32
BF16 = jnp.bfloat16
AHEAD = 2
FAR_FIRST = sorted(range(1, 16), key=lambda k: -min(k // 4, 4 - k // 4) - min(k % 4, 4 - k % 4))


def kernel(acts, grads, pin, pout, qry, lens, mask, out,
           lensv, maskv, av, gv, piv, pov, part, gota, gotb, suma, sumb, fina, finb, zsum, zgot, ksend, kgot, qall, ssend, sgot,
           load_sem, w_sem, s_sem, own_sem, a_send, a_recv, b_send, b_recv, a2_send, a2_recv, b2_send, b2_recv, q_send, q_recv, p_send, p_recv, c_send, c_recv,
           z_send, z_recv, k_send, k_recv, s_send, s_recv, across_in, later_in):
    nt = (((1,), (1,)), ((), ()))
    d = lax.axis_index("dp")
    t = lax.axis_index("tensor")
    zl, c = d // 2, d % 2
    u, zh = t // 2, t % 2
    x, y = u // 4, u % 4
    low = zl % 2
    z = zh * 8 + zl

    def plane(index):
        return {"dp": d, "tensor": 2 * index + zh}

    def around(k):
        return ((x + k // 4) % 4) * 4 + (y + k % 4) % 4

    def column(k):
        zz = (z + k) % 16
        return {"dp": 2 * (zz % 8) + c, "tensor": 2 * u + zz // 8}

    beside = {"dp": 2 * (zl + 1 - 2 * low) + c, "tensor": t}
    sibling = {"dp": 2 * zl + 1 - c, "tensor": t}
    across = {"dp": d, "tensor": 2 * u + 1 - zh}

    def remote(src, dst, send, recv, where):
        pltpu.make_async_remote_copy(
            src_ref=src, dst_ref=dst, send_sem=send, recv_sem=recv, device_id=where, device_id_type=MESH
        ).start()

    def wait(ref, sem):
        pltpu.make_async_copy(ref, ref, sem).wait()

    def loads(i):
        layer, seq = i // 4, i % 4
        rows = pl.ds(pl.multiple_of(seq * 256, 256), 256)
        return (
            pltpu.make_async_copy(acts.at[layer, rows], av.at[i], load_sem.at[0, i]),
            pltpu.make_async_copy(grads.at[layer, rows], gv.at[i], load_sem.at[1, i]),
        )

    barrier = pltpu.get_barrier_semaphore()

    def greet(where):
        pl.semaphore_signal(barrier, inc=1, device_id=where, device_id_type=MESH)

    for k in (1, 2, 3, 4, 8, 12):
        greet(plane(around(k)))

    load_pin = pltpu.make_async_copy(pin, piv, w_sem.at[0])
    load_pout = pltpu.make_async_copy(pout, pov, w_sem.at[1])
    load_pin.start()
    load_pout.start()

    yh, yl = y // 2, y % 2

    def place(q):
        r = q % 4
        step = jnp.where(r == 0, 2, jnp.where(r == 1, 1, jnp.where(r == 2, 3, 0)))
        return (x + step) % 4, jnp.where(q < 4, 1 - yh, yh)

    def start_load(q, carry):
        xb, yb = place(q)
        for copy in loads(2 * xb + yb):
            copy.start()
        return carry

    lax.fori_loop(0, 8, start_load, 0)
    slot = ((2 * c + low) * 2 + zh) * 4 + zl // 2
    own_q = pltpu.make_async_copy(
        qry.at[pl.ds(pl.multiple_of(32 * zh, 32), 32)], qall.at[slot], own_sem
    )
    own_q.start()
    load_lens = pltpu.make_async_copy(lens, lensv, s_sem.at[0])
    load_mask = pltpu.make_async_copy(mask, maskv, s_sem.at[1])
    load_lens.start()
    load_mask.start()

    for k in range(1, 8):

        @pl.when((z + 2 * k) % 16 > z)
        def _():
            greet(column(2 * k))

    @pl.when(low == 0)
    def _():
        greet(beside)

    @pl.when(c == 0)
    def _():
        greet(sibling)

    load_pin.wait()
    load_pout.wait()

    mine = u % 8

    def project(xb, yb):
        i = 2 * xb + yb
        for copy in loads(i):
            copy.wait()
        layer = xb // 2
        inner = lax.dot_general(av[i], piv[layer], nt, preferred_element_type=F32)
        outer = lax.dot_general(gv[i], pov[layer], nt, preferred_element_type=F32)
        part[i, :, :, 0:64] = inner.reshape(4, 64, 64)
        part[i, :, :, 64:128] = outer.reshape(4, 64, 64)

    def give(xb, yb):
        i = 2 * xb + yb

        @pl.when(xb != x)
        def _():
            remote(part.at[i, 0:2], gota.at[x, pl.ds(2 * yb, 2)], a_send, a_recv.at[yb], plane(4 * xb + y))

        for sub in range(2):
            to = 2 * yb + sub

            @pl.when(to != y)
            def _():
                remote(part.at[i, 2 + sub], gotb.at[y, xb], b_send, b_recv.at[xb], plane(4 * x + to))

    def early(q, carry):
        project(*place(q))
        return carry

    lax.fori_loop(0, AHEAD, early, 0)
    pl.semaphore_wait(barrier, 6 + z // 2 + low + c)

    def answer(where, sem):
        pl.semaphore_signal(sem, inc=1, device_id=where, device_id_type=MESH)

    def spread(k):
        far = (z + 2 * k) % 16 // 8
        remote(qry.at[pl.ds(pl.multiple_of(32 * far, 32), 32)], qall.at[slot], q_send, q_recv, column(2 * k))

    @pl.when(z >= 8)
    def _():
        answer(across, across_in)

    for k in range(1, 8):

        @pl.when((z + 2 * k) % 16 < z)
        def _():
            answer(column(2 * k), later_in)
            spread(k)

    @pl.when(low == 1)
    def _():
        answer(beside, later_in)

    @pl.when(c == 1)
    def _():
        answer(sibling, later_in)


    def late(q, carry):
        give(*place(q))
        return carry

    lax.fori_loop(0, AHEAD, late, 0)

    def steady(q, carry):
        project(*place(q))
        give(*place(q))
        return carry

    lax.fori_loop(AHEAD, 8, steady, 0)

    def sum_a(yy):
        total = part[2 * x + yy // 2, yy % 2]
        for k in range(1, 4):
            total = total + gota[(x + k) % 4, yy]
        return total

    def sum_b(xx):
        total = part[2 * xx + yh, 2 + yl]
        for k in range(1, 4):
            total = total + gotb[(y + k) % 4, xx]
        return total

    def pass_a(yy):
        suma[yy] = sum_a(yy)
        remote(suma.at[yy], fina.at[y], a2_send, a2_recv, plane(4 * x + yy))

    def pass_b(xx):
        sumb[xx] = sum_b(xx)
        remote(sumb.at[xx], finb.at[x], b2_send, b2_recv, plane(4 * xx + y))

    later = 9 - z // 2 - low - c

    def meet():
        @pl.when(later > 0)
        def _():
            pl.semaphore_wait(later_in, later)

        for k in range(1, 8):

            @pl.when((z + 2 * k) % 16 > z)
            def _():
                spread(k)

    @pl.when(z >= 4)
    def _():
        meet()

    wait(gota.at[0:3, 0:2], a_recv.at[1 - yh])
    pass_a(2 - 2 * yh)
    pass_a(3 - 2 * yh)
    for step in (2, 1, 3):
        xx = (x + step) % 4
        wait(gotb.at[0:3, 0], b_recv.at[xx])
        pass_b(xx)
    wait(gota.at[0:3, 0:2], a_recv.at[yh])
    pass_a(2 * yh + 1 - yl)

    @pl.when(z < 4)
    def _():
        meet()

    total = sum_a(y)
    wait(fina.at[0:3], a2_recv)
    for k in range(1, 4):
        total = total + fina[(y + k) % 4]
    zsum[0] = total

    @pl.when(z < 8)
    def _():
        pl.semaphore_wait(across_in, 1)

    remote(zsum.at[0], zgot.at[0], z_send.at[0], z_recv.at[0], across)
    wait(gotb.at[0:3, 0], b_recv.at[x])
    total = sum_b(x)
    wait(finb.at[0:3], b2_recv)
    for k in range(1, 4):
        total = total + finb[(x + k) % 4]
    zsum[1] = total
    remote(zsum.at[1], zgot.at[1], z_send.at[1], z_recv.at[1], across)

    own_q.wait()
    wait(qall.at[0:7], q_recv)
    column_half = qall.at[pl.ds(16 * c + 8 * low, 8)]
    remote(column_half, column_half, p_send, p_recv, beside)
    remote(column_half, column_half, c_send.at[0], c_recv.at[0], sibling)

    load_lens.wait()
    load_mask.wait()
    seq = (u // 2) % 4
    lane = lax.broadcasted_iota(jnp.int32, (128, 128), 1)
    lane4 = lane[:4]
    low4 = lane4 < 64
    first, second = maskv[:, :128], maskv[:, 128:]
    even = jnp.where(low4, first, pltpu.roll(second, 64, 1))
    odd = jnp.where(low4, pltpu.roll(first, 64, 1), second)
    marks = jnp.where(lax.broadcasted_iota(jnp.int32, (4, 128), 0) == seq, jnp.where(yl == 0, even, odd), 0)
    counted = jnp.sum(marks, axis=0, keepdims=True)
    slots = lane[:1] + 64 * yl + jnp.where(lane[:1] < 64, 0, 64)
    live = jnp.where(slots < lensv[seq], counted, 0).astype(F32)

    def part_kron(h):
        unit = zsum[h] + zgot[h]
        weighted = unit.T[64:128] * live[:, 64 * h : 64 * h + 64]
        twice = jnp.where(lane[:64] < 64, unit, pltpu.roll(unit, 64, 1))
        wh, th = weighted.astype(BF16), twice.astype(BF16)
        wl, tl = (weighted - wh.astype(F32)).astype(BF16), (twice - th.astype(F32)).astype(BF16)
        return (
            jnp.dot(wh, th, preferred_element_type=F32)
            + jnp.dot(wh, tl, preferred_element_type=F32)
            + jnp.dot(wl, th, preferred_element_type=F32)
        )

    wait(gota.at[0:3], a_send)
    wait(gotb.at[0:3], b_send)
    wait(fina.at[0:3], a2_send)
    wait(finb.at[0:3], b2_send)
    wait(qall.at[0:7], q_send)
    wait(zgot.at[0], z_recv.at[0])
    kron = part_kron(0)
    wait(zgot.at[1], z_recv.at[1])
    kron = kron + part_kron(1)
    ksend[...] = kron.reshape(8, 8, 128)
    for dx, dy in ((1, 2), (0, 2), (1, 1), (1, 3), (0, 1), (0, 3), (1, 0)):
        to = (x + dx) % 2 * 4 + (y + dy) % 4
        remote(ksend.at[to], kgot.at[mine], k_send, k_recv, plane((u // 8) * 8 + to))
    kgot[mine] = ksend[mine]
    wait(qall.at[0:8], p_recv)
    other_half = qall.at[pl.ds(16 * c + 8 - 8 * low, 8)]
    remote(other_half, other_half, c_send.at[1], c_recv.at[1], sibling)
    wait(kgot.at[0:7], k_recv)
    for h in range(2):
        wait(qall.at[0:8], c_recv.at[h])
    rows8 = []
    for s in range(4):
        rows8.append(kgot[2 * s] + kgot[2 * s + 1])
    stacked = jnp.stack(rows8, axis=0)
    flat = jnp.concatenate(
        [jnp.where(low4, stacked[:, 2 * r, :], stacked[:, 2 * r + 1, :]) for r in range(4)], axis=1
    )
    flat = jnp.concatenate([flat, jnp.zeros_like(flat)], axis=0).astype(BF16)
    for m in range(4):
        ssend[m] = sum(
            lax.dot_general(
                flat[:, 256 * e : 256 * e + 256], qall[8 * m + 4 * e : 8 * m + 4 * e + 4].reshape(128, 256), nt,
                preferred_element_type=F32,
            )
            for e in range(2)
        )
    for k in FAR_FIRST:
        to = around(k)
        remote(ssend.at[to % 2 * 2 + to // 2 % 2], sgot.at[k - 1], s_send, s_recv, plane(to))
    for h in range(2):
        wait(zgot.at[h], z_send.at[h])
    wait(qall.at[0:8], p_send)
    for h in range(2):
        wait(qall.at[0:8], c_send.at[h])
    wait(kgot.at[0:7], k_send)
    wait(sgot, s_recv)
    total = ssend[u % 2 * 2 + u // 2 % 2]
    for k in range(15):
        total = total + sgot[k]
    result = jnp.zeros((4, 32), F32)
    for g in range(4):
        result = result + jnp.where(x == g, total[:4, 32 * g : 32 * g + 32], 0.0)
    out[...] = result
    wait(sgot, s_send)


def on_device(acts, grads, proj_in, proj_out, queries, lengths, loss_mask):
    hbm = pl.BlockSpec(memory_space=pltpu.HBM)
    vmem = pl.BlockSpec(memory_space=pltpu.VMEM)
    dma = pltpu.SemaphoreType.DMA
    ff, dm = acts.shape[2], grads.shape[2]
    return pl.pallas_call(
        kernel,
        out_shape=jax.ShapeDtypeStruct((4, 32), F32),
        in_specs=[hbm] * 7,
        out_specs=vmem,
        scratch_shapes=[
            pltpu.SMEM((4,), jnp.int32),
            pltpu.VMEM((4, 256), jnp.int32),
            pltpu.VMEM((8, 256, ff), BF16),
            pltpu.VMEM((8, 256, dm), BF16),
            pltpu.VMEM((2, 64, ff), BF16),
            pltpu.VMEM((2, 64, dm), BF16),
            pltpu.VMEM((8, 4, 64, 128), F32),
            pltpu.VMEM((4, 4, 64, 128), F32),
            pltpu.VMEM((4, 4, 64, 128), F32),
            pltpu.VMEM((4, 64, 128), F32),
            pltpu.VMEM((4, 64, 128), F32),
            pltpu.VMEM((4, 64, 128), F32),
            pltpu.VMEM((4, 64, 128), F32),
            pltpu.VMEM((2, 64, 128), F32),
            pltpu.VMEM((2, 64, 128), F32),
            pltpu.VMEM((8, 8, 128), F32),
            pltpu.VMEM((8, 8, 128), F32),
            pltpu.VMEM((32, 32, 256), BF16),
            pltpu.VMEM((4, 8, 128), F32),
            pltpu.VMEM((15, 8, 128), F32),
            dma((2, 8)), dma((2,)), dma((2,)), dma,
            dma, dma((2,)), dma, dma((4,)), dma, dma, dma, dma, dma, dma, dma, dma, dma((2,)), dma((2,)),
            dma((2,)), dma((2,)), dma, dma, dma, dma,
            pltpu.SemaphoreType.REGULAR, pltpu.SemaphoreType.REGULAR,
        ],
        compiler_params=pltpu.CompilerParams(
            collective_id=0, has_side_effects=True, vmem_limit_bytes=60 << 20
        ),
        cost_estimate=pl.CostEstimate(flops=310_000_000, bytes_accessed=6_000_000, transcendentals=0),
        name="attribute",
    )(acts, grads, proj_in.transpose(0, 2, 1), proj_out.transpose(0, 2, 1), queries, lengths, loss_mask)


def solution(mesh):
    placed = (
        P(None, "dp", "tensor"),
        P(None, "dp", "tensor"),
        P(None, "tensor", None),
        P(None, "tensor", None),
        P("dp", "tensor"),
        P("dp"),
        P("dp", None),
    )
    return jax.shard_map(
        on_device, mesh=mesh, in_specs=placed, out_specs=P("dp", "tensor"), check_vma=False
    )
```

```python
import jax
import jax.numpy as jnp
from jax import lax
from jax.experimental import pallas as pl
from jax.experimental.pallas import tpu as pltpu
from jax.sharding import PartitionSpec as P

MESH = pl.DeviceIdType.MESH
F32 = jnp.float32
BF16 = jnp.bfloat16
AHEAD = 2


def kernel(acts, grads, pin, pout, qry, lens, mask, out,
           lensv, maskv, av, gv, piv, pov, part, gota, gotb, suma, sumb, fina, finb, zsum, zgot, ksend, kgot, qall, ssend, sgot,
           load_sem, w_sem, s_sem, own_sem, a_send, a_recv, b_send, b_recv, a2_send, a2_recv, b2_send, b2_recv, q_send, q_recv, p_send, p_recv, c_send, c_recv,
           z_send, z_recv, k_send, k_recv, s_send, s_recv, across_in, later_in):
    nt = (((1,), (1,)), ((), ()))
    d = lax.axis_index("dp")
    t = lax.axis_index("tensor")
    zl, c = d // 2, d % 2
    u, zh = t // 2, t % 2
    x, y = u // 4, u % 4
    low = zl % 2
    z = zh * 8 + zl

    def plane(index):
        return {"dp": d, "tensor": 2 * index + zh}

    def around(k):
        return ((x + k // 4) % 4) * 4 + (y + k % 4) % 4

    def column(k):
        zz = (z + k) % 16
        return {"dp": 2 * (zz % 8) + c, "tensor": 2 * u + zz // 8}

    beside = {"dp": 2 * (zl + 1 - 2 * low) + c, "tensor": t}
    sibling = {"dp": 2 * zl + 1 - c, "tensor": t}
    across = {"dp": d, "tensor": 2 * u + 1 - zh}

    def remote(src, dst, send, recv, where):
        pltpu.make_async_remote_copy(
            src_ref=src, dst_ref=dst, send_sem=send, recv_sem=recv, device_id=where, device_id_type=MESH
        ).start()

    def wait(ref, sem):
        pltpu.make_async_copy(ref, ref, sem).wait()

    def loads(i):
        layer, seq = i // 4, i % 4
        rows = pl.ds(pl.multiple_of(seq * 256, 256), 256)
        return (
            pltpu.make_async_copy(acts.at[layer, rows], av.at[i], load_sem.at[0, i]),
            pltpu.make_async_copy(grads.at[layer, rows], gv.at[i], load_sem.at[1, i]),
        )

    barrier = pltpu.get_barrier_semaphore()

    def greet(where):
        pl.semaphore_signal(barrier, inc=1, device_id=where, device_id_type=MESH)

    for k in (1, 2, 3, 4, 8, 12):
        greet(plane(around(k)))

    load_pin = pltpu.make_async_copy(pin, piv, w_sem.at[0])
    load_pout = pltpu.make_async_copy(pout, pov, w_sem.at[1])
    load_pin.start()
    load_pout.start()

    yh, yl = y // 2, y % 2

    def place(q):
        r = q % 4
        step = jnp.where(r == 0, 2, jnp.where(r == 1, 1, jnp.where(r == 2, 3, 0)))
        return (x + step) % 4, jnp.where(q < 4, 1 - yh, yh)

    def start_load(q, carry):
        xb, yb = place(q)
        for copy in loads(2 * xb + yb):
            copy.start()
        return carry

    lax.fori_loop(0, 8, start_load, 0)
    slot = ((2 * c + low) * 2 + zh) * 4 + zl // 2
    own_q = pltpu.make_async_copy(
        qry.at[pl.ds(pl.multiple_of(32 * zh, 32), 32)], qall.at[slot], own_sem
    )
    own_q.start()
    load_lens = pltpu.make_async_copy(lens, lensv, s_sem.at[0])
    load_mask = pltpu.make_async_copy(mask, maskv, s_sem.at[1])
    load_lens.start()
    load_mask.start()

    for k in range(1, 8):

        @pl.when((z + 2 * k) % 16 > z)
        def _():
            greet(column(2 * k))

    @pl.when(low == 0)
    def _():
        greet(beside)

    @pl.when(c == 0)
    def _():
        greet(sibling)

    load_pin.wait()
    load_pout.wait()

    mine = u % 8

    def project(xb, yb):
        i = 2 * xb + yb
        for copy in loads(i):
            copy.wait()
        layer = xb // 2
        inner = lax.dot_general(av[i], piv[layer], nt, preferred_element_type=F32)
        outer = lax.dot_general(gv[i], pov[layer], nt, preferred_element_type=F32)
        part[i, :, :, 0:64] = inner.reshape(4, 64, 64)
        part[i, :, :, 64:128] = outer.reshape(4, 64, 64)

    def give(xb, yb):
        i = 2 * xb + yb

        @pl.when(xb != x)
        def _():
            remote(part.at[i, 0:2], gota.at[x, pl.ds(2 * yb, 2)], a_send, a_recv.at[yb], plane(4 * xb + y))

        for sub in range(2):
            to = 2 * yb + sub

            @pl.when(to != y)
            def _():
                remote(part.at[i, 2 + sub], gotb.at[y, xb], b_send, b_recv.at[xb], plane(4 * x + to))

    def early(q, carry):
        project(*place(q))
        return carry

    lax.fori_loop(0, AHEAD, early, 0)
    pl.semaphore_wait(barrier, 6 + z // 2 + low + c)

    def answer(where, sem):
        pl.semaphore_signal(sem, inc=1, device_id=where, device_id_type=MESH)

    def spread(k):
        far = (z + 2 * k) % 16 // 8
        remote(qry.at[pl.ds(pl.multiple_of(32 * far, 32), 32)], qall.at[slot], q_send, q_recv, column(2 * k))

    @pl.when(z >= 8)
    def _():
        answer(across, across_in)

    for k in range(1, 8):

        @pl.when((z + 2 * k) % 16 < z)
        def _():
            answer(column(2 * k), later_in)
            spread(k)

    @pl.when(low == 1)
    def _():
        answer(beside, later_in)

    @pl.when(c == 1)
    def _():
        answer(sibling, later_in)


    def late(q, carry):
        give(*place(q))
        return carry

    lax.fori_loop(0, AHEAD, late, 0)

    def steady(q, carry):
        project(*place(q))
        give(*place(q))
        return carry

    lax.fori_loop(AHEAD, 8, steady, 0)

    def sum_a(yy):
        total = part[2 * x + yy // 2, yy % 2]
        for k in range(1, 4):
            total = total + gota[(x + k) % 4, yy]
        return total

    def sum_b(xx):
        total = part[2 * xx + yh, 2 + yl]
        for k in range(1, 4):
            total = total + gotb[(y + k) % 4, xx]
        return total

    def pass_a(yy):
        suma[yy] = sum_a(yy)
        remote(suma.at[yy], fina.at[y], a2_send, a2_recv, plane(4 * x + yy))

    def pass_b(xx):
        sumb[xx] = sum_b(xx)
        remote(sumb.at[xx], finb.at[x], b2_send, b2_recv, plane(4 * xx + y))

    later = 9 - z // 2 - low - c

    def meet():
        @pl.when(later > 0)
        def _():
            pl.semaphore_wait(later_in, later)

        for k in range(1, 8):

            @pl.when((z + 2 * k) % 16 > z)
            def _():
                spread(k)

    @pl.when(z >= 4)
    def _():
        meet()

    wait(gota.at[0:3, 0:2], a_recv.at[1 - yh])
    pass_a(2 - 2 * yh)
    pass_a(3 - 2 * yh)
    for step in (2, 1, 3):
        xx = (x + step) % 4
        wait(gotb.at[0:3, 0], b_recv.at[xx])
        pass_b(xx)
    wait(gota.at[0:3, 0:2], a_recv.at[yh])
    pass_a(2 * yh + 1 - yl)

    @pl.when(z < 4)
    def _():
        meet()

    total = sum_a(y)
    wait(fina.at[0:3], a2_recv)
    for k in range(1, 4):
        total = total + fina[(y + k) % 4]
    zsum[0] = total

    @pl.when(z < 8)
    def _():
        pl.semaphore_wait(across_in, 1)

    remote(zsum.at[0], zgot.at[0], z_send.at[0], z_recv.at[0], across)
    wait(gotb.at[0:3, 0], b_recv.at[x])
    total = sum_b(x)
    wait(finb.at[0:3], b2_recv)
    for k in range(1, 4):
        total = total + finb[(x + k) % 4]
    zsum[1] = total
    remote(zsum.at[1], zgot.at[1], z_send.at[1], z_recv.at[1], across)

    own_q.wait()
    wait(qall.at[0:7], q_recv)
    column_half = qall.at[pl.ds(16 * c + 8 * low, 8)]
    remote(column_half, column_half, p_send, p_recv, beside)
    remote(column_half, column_half, c_send.at[0], c_recv.at[0], sibling)

    load_lens.wait()
    load_mask.wait()
    seq = (u // 2) % 4
    lane = lax.broadcasted_iota(jnp.int32, (128, 128), 1)
    lane4 = lane[:4]
    low4 = lane4 < 64
    first, second = maskv[:, :128], maskv[:, 128:]
    even = jnp.where(low4, first, pltpu.roll(second, 64, 1))
    odd = jnp.where(low4, pltpu.roll(first, 64, 1), second)
    marks = jnp.where(lax.broadcasted_iota(jnp.int32, (4, 128), 0) == seq, jnp.where(yl == 0, even, odd), 0)
    counted = jnp.sum(marks, axis=0, keepdims=True)
    slots = lane[:1] + 64 * yl + jnp.where(lane[:1] < 64, 0, 64)
    live = jnp.where(slots < lensv[seq], counted, 0).astype(F32)

    def part_kron(h):
        unit = zsum[h] + zgot[h]
        weighted = unit.T[64:128] * live[:, 64 * h : 64 * h + 64]
        twice = jnp.where(lane[:64] < 64, unit, pltpu.roll(unit, 64, 1))
        wh, th = weighted.astype(BF16), twice.astype(BF16)
        wl, tl = (weighted - wh.astype(F32)).astype(BF16), (twice - th.astype(F32)).astype(BF16)
        return (
            jnp.dot(wh, th, preferred_element_type=F32)
            + jnp.dot(wh, tl, preferred_element_type=F32)
            + jnp.dot(wl, th, preferred_element_type=F32)
        )

    wait(gota.at[0:3], a_send)
    wait(gotb.at[0:3], b_send)
    wait(fina.at[0:3], a2_send)
    wait(finb.at[0:3], b2_send)
    wait(qall.at[0:7], q_send)
    wait(zgot.at[0], z_recv.at[0])
    kron = part_kron(0)
    wait(zgot.at[1], z_recv.at[1])
    kron = kron + part_kron(1)
    ksend[...] = kron.reshape(8, 8, 128)
    for dx, dy in ((1, 2), (0, 2), (1, 1), (1, 3), (0, 1), (0, 3), (1, 0)):
        to = (x + dx) % 2 * 4 + (y + dy) % 4
        remote(ksend.at[to], kgot.at[mine], k_send, k_recv, plane((u // 8) * 8 + to))
    kgot[mine] = ksend[mine]
    wait(qall.at[0:8], p_recv)
    other_half = qall.at[pl.ds(16 * c + 8 - 8 * low, 8)]
    remote(other_half, other_half, c_send.at[1], c_recv.at[1], sibling)
    wait(kgot.at[0:7], k_recv)
    for h in range(2):
        wait(qall.at[0:8], c_recv.at[h])
    rows8 = []
    for s in range(4):
        rows8.append(kgot[2 * s] + kgot[2 * s + 1])
    stacked = jnp.stack(rows8, axis=0)
    flat = jnp.concatenate(
        [jnp.where(low4, stacked[:, 2 * r, :], stacked[:, 2 * r + 1, :]) for r in range(4)], axis=1
    )
    flat = jnp.concatenate([flat, jnp.zeros_like(flat)], axis=0).astype(BF16)
    for m in range(4):
        ssend[m] = sum(
            lax.dot_general(
                flat[:, 256 * e : 256 * e + 256], qall[8 * m + 4 * e : 8 * m + 4 * e + 4].reshape(128, 256), nt,
                preferred_element_type=F32,
            )
            for e in range(2)
        )
        for step in (2, 1, 3, 0):
            to = 4 * ((x + step) % 4) + 2 * (m % 2) + m // 2

            @pl.when(to != u)
            def _():
                remote(ssend.at[m], sgot.at[u], s_send, s_recv, plane(to))

    for h in range(2):
        wait(zgot.at[h], z_send.at[h])
    wait(qall.at[0:8], p_send)
    for h in range(2):
        wait(qall.at[0:8], c_send.at[h])
    wait(kgot.at[0:7], k_send)
    wait(sgot.at[0:15], s_recv)
    total = ssend[u % 2 * 2 + u // 2 % 2]
    for k in range(1, 16):
        total = total + sgot[(u + k) % 16]
    result = jnp.zeros((4, 32), F32)
    for g in range(4):
        result = result + jnp.where(x == g, total[:4, 32 * g : 32 * g + 32], 0.0)
    out[...] = result
    wait(sgot.at[0:15], s_send)


def on_device(acts, grads, proj_in, proj_out, queries, lengths, loss_mask):
    hbm = pl.BlockSpec(memory_space=pltpu.HBM)
    vmem = pl.BlockSpec(memory_space=pltpu.VMEM)
    dma = pltpu.SemaphoreType.DMA
    ff, dm = acts.shape[2], grads.shape[2]
    return pl.pallas_call(
        kernel,
        out_shape=jax.ShapeDtypeStruct((4, 32), F32),
        in_specs=[hbm] * 7,
        out_specs=vmem,
        scratch_shapes=[
            pltpu.SMEM((4,), jnp.int32),
            pltpu.VMEM((4, 256), jnp.int32),
            pltpu.VMEM((8, 256, ff), BF16),
            pltpu.VMEM((8, 256, dm), BF16),
            pltpu.VMEM((2, 64, ff), BF16),
            pltpu.VMEM((2, 64, dm), BF16),
            pltpu.VMEM((8, 4, 64, 128), F32),
            pltpu.VMEM((4, 4, 64, 128), F32),
            pltpu.VMEM((4, 4, 64, 128), F32),
            pltpu.VMEM((4, 64, 128), F32),
            pltpu.VMEM((4, 64, 128), F32),
            pltpu.VMEM((4, 64, 128), F32),
            pltpu.VMEM((4, 64, 128), F32),
            pltpu.VMEM((2, 64, 128), F32),
            pltpu.VMEM((2, 64, 128), F32),
            pltpu.VMEM((8, 8, 128), F32),
            pltpu.VMEM((8, 8, 128), F32),
            pltpu.VMEM((32, 32, 256), BF16),
            pltpu.VMEM((4, 8, 128), F32),
            pltpu.VMEM((16, 8, 128), F32),
            dma((2, 8)), dma((2,)), dma((2,)), dma,
            dma, dma((2,)), dma, dma((4,)), dma, dma, dma, dma, dma, dma, dma, dma, dma((2,)), dma((2,)),
            dma((2,)), dma((2,)), dma, dma, dma, dma,
            pltpu.SemaphoreType.REGULAR, pltpu.SemaphoreType.REGULAR,
        ],
        compiler_params=pltpu.CompilerParams(
            collective_id=0, has_side_effects=True, vmem_limit_bytes=60 << 20
        ),
        cost_estimate=pl.CostEstimate(flops=310_000_000, bytes_accessed=6_000_000, transcendentals=0),
        name="attribute",
    )(acts, grads, proj_in.transpose(0, 2, 1), proj_out.transpose(0, 2, 1), queries, lengths, loss_mask)


def solution(mesh):
    placed = (
        P(None, "dp", "tensor"),
        P(None, "dp", "tensor"),
        P(None, "tensor", None),
        P(None, "tensor", None),
        P("dp", "tensor"),
        P("dp"),
        P("dp", None),
    )
    return jax.shard_map(
        on_device, mesh=mesh, in_specs=placed, out_specs=P("dp", "tensor"), check_vma=False
    )
```
